256 devices in a mesh: dp: 2 (over z_lo), fsdp: 8 (over x, core), ctx: 16 (over y, z_hi).
Axes of the slice: x: 4, y: 4, z: 8 (z_hi: 4, z_lo: 2; z = z_hi * 2 + z_lo), core: 2. Of those that a mesh axis runs over, the one named last changes fastest.
Arguments:
- queries: bfloat16 [16, 2048, 1792], P(('dp', 'fsdp'), 'ctx'), may hold values from -56 to 56
- key_states: bfloat16 [16, 2048, 256], P(('dp', 'fsdp'), 'ctx'), may hold values from -16 to 16
- value_states: bfloat16 [16, 2048, 256], P(('dp', 'fsdp'), 'ctx'), may hold values from -6 to 6
- out_grad: bfloat16 [16, 2048, 1792], P(('dp', 'fsdp'), 'ctx'), may hold values from -6 to 6
- layer_input: bfloat16 [16, 2048, 3584], P(('dp', 'fsdp'), 'ctx'), may hold values from -6 to 6
- segment_ids: int32 [16, 2048], P(('dp', 'fsdp')), may hold values from 0 to 2, never falling along the last dimension, each value on 1 to 1536 neighbouring positions
Outputs:
- query_grad: bfloat16 [16, 2048, 1792], P(('dp', 'fsdp'), 'ctx')
- key_grad: bfloat16 [16, 2048, 256], P(('dp', 'fsdp'), 'ctx')
- value_grad: bfloat16 [16, 2048, 256], P(('dp', 'fsdp'), 'ctx')
- weight_grad: float32 [3584, 512], P('fsdp')
The draws below stay inside these ranges and needn't reach their ends.
All inputs are finite; a program needn't handle non-finite values.
Results may differ from the reference program's by a relative error of at most 0.025.
Values may be sent and summed in bfloat16 or wider, within the bound.
No kernel may reach another device: no remote copies, remote signals or barrier semaphores. Data moves between devices by JAX's collectives and lax.ppermute only.
A program may use at most 128 MiB of HBM per device.

```python
import math
import jax
import jax.numpy as jnp
import numpy as np
from jax import lax

D = 3584
H = 14
KVH = 2
HD = 128
SEQ = 2048
ROWS = 16
TOKENS = 32768


def draw_key_states(key, part):
    key = jax.random.fold_in(key, 11)
    noise = jnp.clip(jax.random.normal(key, (ROWS, SEQ, KVH * HD), jnp.float32), -6.0, 6.0)
    return noise.astype(jnp.bfloat16)


def draw_queries(key, part):
    key = jax.random.fold_in(key, 23)
    noise_key = jax.random.fold_in(key, 0)
    noise = jnp.clip(jax.random.normal(noise_key, (ROWS, SEQ, KVH, H // KVH, HD), jnp.float32), -6.0, 6.0)
    return noise.reshape(ROWS, SEQ, H * HD).astype(jnp.bfloat16)


def spiked(entries, key, source, target, blocks, factor):
    owner, partner = [(jnp.arange(entries.shape[axis_at]) // (entries.shape[axis_at] // blocks)).reshape([-1 if axis == axis_at else 1 for axis in range(entries.ndim)]) for axis_at in (source, target)]
    chosen = jax.random.permutation(key, blocks)[partner]
    strong = (owner == chosen) | (owner == (partner + blocks // 2) % blocks)
    return jnp.where(strong, factor * entries, entries)


def block_levels(own_key, shape, cuts, least, largest):
    def one(position, blocks):
        heights = jax.random.uniform(jax.random.fold_in(jax.random.fold_in(own_key, 6), position), (blocks,), jnp.float32, least / len(cuts), largest / len(cuts))
        return jnp.repeat(jnp.exp(heights), shape[position] // blocks).reshape((-1,) + (1,) * (len(shape) - position - 1))

    gain = one(*cuts[0])
    for cut in cuts[1:]:
        gain = gain * one(*cut)
    return gain


def length_profile(count, total, bound, skew):
    loads = [(1 << 20) // math.isqrt(rank ** skew) + 1 for rank in range(2, count + 1)]
    rest, holding = total - bound - (count - 1), [1] * (count - 1)
    while rest > 0:
        candidates = [i for i in range(count - 1) if holding[i] < bound]
        mass, left = sum([loads[i] for i in candidates]), rest
        for i in candidates:
            more = min(bound - holding[i], max(1, left * loads[i] // mass), rest)
            holding[i] = holding[i] + more
            rest = rest - more
    return np.array([bound] + holding)


def uneven_parts(stream_key, number_of, total, bound, lean):
    if number_of == 2:
        one = jax.random.randint(stream_key, (), max(1, total - bound), min(bound, total - 1) + 1)
        return jnp.stack([one, total - one])
    tallies = jnp.asarray(length_profile(number_of, total, bound, lean), jnp.int32)
    couples = (number_of - 1) // 2
    giver, taker = tallies[1:1 + 2 * couples:2], tallies[2:2 + 2 * couples:2]
    margin = jnp.minimum(giver - 1, bound - taker)
    moved = jax.random.randint(jax.random.fold_in(stream_key, 1), (couples,), 0, 1 << 20) % (margin + 1)
    tallies = tallies.at[1:1 + 2 * couples:2].set(giver - moved).at[2:2 + 2 * couples:2].set(taker + moved)
    return tallies[jax.random.permutation(jax.random.fold_in(stream_key, 2), number_of)]


def normal_values(rng, extent, width, limit, shards=(), held_as=jnp.bfloat16):
    gain = block_levels(rng, extent, shards, -0.22, 0.18) if shards else 1.0
    result = jax.random.normal(rng, extent, jnp.float32) * width * gain
    return jnp.minimum(jnp.maximum(result, -limit), limit).astype(held_as)


def noise_with(own_key, shape, spread, bound, shards, heavy, kind=jnp.bfloat16):
    entries = spread * jax.random.normal(own_key, shape, jnp.float32)
    if shards:
        entries = entries * block_levels(own_key, shape, shards, -0.22, 0.18)
    return jnp.clip(spiked(entries, jax.random.fold_in(own_key, 3), *heavy), -bound, bound).astype(kind)


def setup_inputs(seed: int = 0) -> dict:
    streams_of = jax.random.split(jax.random.key(seed), 7)
    queries = draw_queries(jax.random.fold_in(streams_of[6], 71), 0)
    key_states = draw_key_states(jax.random.fold_in(streams_of[6], 71), 0)
    value_states = normal_values(streams_of[2], (ROWS, SEQ, KVH * HD), 1.0, 6.0, ((0, 16), (1, 16)))
    out_grad = normal_values(streams_of[3], (ROWS, SEQ, H * HD), 1.0, 6.0, ((0, 16), (1, 16)))
    layer_input = noise_with(streams_of[4], (ROWS, SEQ, D), 1.0, 6.0, ((0, 16), (1, 16)), (1, 2, 16, 2.0))
    segment_ids = jax.vmap(lambda own: jnp.searchsorted(jnp.cumsum(uneven_parts(own, 3, SEQ, 3 * SEQ // 4, 0)), jnp.arange(SEQ), side="right"))(jax.random.split(streams_of[5], ROWS)).reshape((ROWS, SEQ)).astype(jnp.int32)
    return {"queries": queries, "key_states": key_states, "value_states": value_states, "out_grad": out_grad, "layer_input": layer_input, "segment_ids": segment_ids}


def group_backward(group_queries, group_keys, group_values, group_out, visible):
    softmax_scale = HD ** -0.5
    scores = jnp.einsum("tpd,kd->tpk", group_queries.astype(jnp.float32), group_keys.astype(jnp.float32)) * softmax_scale
    scores = jnp.where(visible[:, None, :], scores, -jnp.inf)
    row_max = jnp.max(scores, axis=-1, keepdims=True)
    shifted = jnp.exp(scores - row_max)
    weights = shifted / jnp.sum(shifted, axis=-1, keepdims=True)
    weights_low = weights.astype(jnp.bfloat16)
    outputs = jnp.einsum("tpk,kd->tpd", weights_low.astype(jnp.float32), group_values.astype(jnp.float32))
    deltas = jnp.sum(group_out.astype(jnp.float32) * outputs, axis=-1, keepdims=True)
    prob_grad = jnp.einsum("tpd,kd->tpk", group_out.astype(jnp.float32), group_values.astype(jnp.float32))
    score_grad = (weights * (prob_grad - deltas) * softmax_scale).astype(jnp.bfloat16)
    query_part = jnp.einsum("tpk,kd->tpd", score_grad.astype(jnp.float32), group_keys.astype(jnp.float32))
    key_part = jnp.einsum("tpk,tpd->kd", score_grad.astype(jnp.float32), group_queries.astype(jnp.float32))
    value_part = jnp.einsum("tpk,tpd->kd", weights_low.astype(jnp.float32), group_out.astype(jnp.float32))
    return query_part, key_part, value_part


def row_backward(items):
    row_queries, row_keys, row_values, row_out, row_segments = items
    group_size = H // KVH
    positions = jnp.arange(SEQ, dtype=jnp.int32)
    visible = (row_segments[:, None] == row_segments[None, :]) & (positions[None, :] <= positions[:, None])
    query_parts = []
    key_parts = []
    value_parts = []
    for group in range(KVH):
        left = group * group_size * HD
        right = (group + 1) * group_size * HD
        group_queries = row_queries[:, left:right].reshape(SEQ, group_size, HD)
        group_out = row_out[:, left:right].reshape(SEQ, group_size, HD)
        group_keys = row_keys[:, group * HD:(group + 1) * HD]
        group_values = row_values[:, group * HD:(group + 1) * HD]
        query_part, key_part, value_part = group_backward(group_queries, group_keys, group_values, group_out, visible)
        query_parts.append(query_part.reshape(SEQ, group_size * HD))
        key_parts.append(key_part)
        value_parts.append(value_part)
    query_grad = jnp.concatenate(query_parts, axis=1).astype(jnp.bfloat16)
    key_grad = jnp.concatenate(key_parts, axis=1).astype(jnp.bfloat16)
    value_grad = jnp.concatenate(value_parts, axis=1).astype(jnp.bfloat16)
    return query_grad, key_grad, value_grad


def reference(queries, key_states, value_states, out_grad, layer_input, segment_ids):
    query_grad, key_grad, value_grad = lax.map(row_backward, (queries, key_states, value_states, out_grad, segment_ids))
    joined = jnp.concatenate([key_grad, value_grad], axis=2).reshape(TOKENS, 2 * KVH * HD)
    flat_input = layer_input.reshape(TOKENS, D)
    weight_grad = jnp.dot(flat_input.T, joined, preferred_element_type=jnp.float32) * (TOKENS ** -0.5)
    return query_grad, key_grad, value_grad, weight_grad
```

```python
import jax
import jax.numpy as jnp
from jax import lax
from jax.experimental import pallas as pl
from jax.experimental.pallas import tpu as pltpu
from jax.sharding import Mesh, PartitionSpec as P

HD = 128
GROUPS = 2
GS = 7
BLK = 128
KT = 256
LOG2E = 1.4426950408889634
SCALE = HD ** (-0.5)

DP, FX, FC, YH, YL, Z = "dp", "fx", "fc", "yh", "yl", "zh"
FSDP = (FX, FC)
YAX = (YH, YL)
CTX = (YH, YL, Z)
PARTNER = [(0, 3), (3, 0), (1, 2), (2, 1)]
NEIGHBOUR = [(0, 1), (1, 0), (2, 3), (3, 2)]


def attention_kernel(
    sc_ref, seg_ref, own_ref, recv_ref, kv_ref,
    dq_own_ref, dq_recv_ref, mine_ref, theirs_ref,
    s_ref, dp_ref, kt_ref, acc_ref, dqt_ref,
):
    length = kv_ref.shape[0]
    tiles = length // KT
    rows = GS * BLK
    nt = (((1,), (1,)), ((), ()))
    nn = (((1,), (0,)), ((), ()))
    f32 = jnp.float32
    bf16 = jnp.bfloat16
    seg = seg_ref[...]
    first = jnp.sum((seg < 1).astype(f32)).astype(jnp.int32)
    second = jnp.sum((seg < 2).astype(f32)).astype(jnp.int32)
    for t in range(tiles):
        kt_ref[t] = kv_ref[t * KT:(t + 1) * KT, 0:HD].T
    acc_ref[...] = jnp.zeros_like(acc_ref)

    def stack(ref, at):
        return jnp.concatenate(
            [ref[at * BLK:(at + 1) * BLK, h * HD:(h + 1) * HD] for h in range(GS)], axis=0
        )

    def block(src_ref, dq_ref, p0):
        qs = stack(src_ref, 0)
        dos = stack(src_ref, 1)
        qpos = p0 + lax.broadcasted_iota(jnp.int32, (1, BLK), 1)
        start = jnp.where(qpos >= second, second, jnp.where(qpos >= first, first, 0))
        low = jnp.where(p0 >= second, second, jnp.where(p0 >= first, first, 0))
        lo = low // KT
        hi = p0 // KT + 1

        def score(t, m):
            at = pl.multiple_of(t * KT, KT)
            k = kv_ref[pl.ds(at, KT), 0:HD]
            s = lax.dot_general(k, qs, nt, preferred_element_type=f32)
            kpos = at + lax.broadcasted_iota(jnp.int32, (KT, BLK), 0)
            seen = (kpos >= start) & (kpos <= qpos)
            s = jnp.concatenate(
                [jnp.where(seen, s[:, h * BLK:(h + 1) * BLK], -jnp.inf) for h in range(GS)], axis=1
            )
            s_ref[pl.ds(at, KT), :] = s
            return jnp.maximum(m, jnp.max(s, axis=0, keepdims=True))

        m = lax.fori_loop(lo, hi, score, jnp.full((1, rows), -jnp.inf, f32))

        def soft(t, carry):
            total, dot = carry
            at = pl.multiple_of(t * KT, KT)
            p = jnp.exp2((s_ref[pl.ds(at, KT), :] - m) * (SCALE * LOG2E))
            v = kv_ref[pl.ds(at, KT), HD:2 * HD]
            dp = lax.dot_general(v, dos, nt, preferred_element_type=f32)
            s_ref[pl.ds(at, KT), :] = p
            dp_ref[pl.ds(at, KT), :] = dp
            total = total + jnp.sum(p, axis=0, keepdims=True)
            dot = dot + jnp.sum(p * dp, axis=0, keepdims=True)
            return total, dot

        zero = jnp.zeros((1, rows), f32)
        total, dot = lax.fori_loop(lo, hi, soft, (zero, zero))
        inv = 1.0 / total
        delta = dot * inv
        inv_scaled = inv * SCALE
        dqt_ref[...] = jnp.zeros_like(dqt_ref)

        def grads(t, carry):
            at = pl.multiple_of(t * KT, KT)
            p = s_ref[pl.ds(at, KT), :]
            w = (p * inv).astype(bf16)
            ds = (p * (dp_ref[pl.ds(at, KT), :] - delta) * inv_scaled).astype(bf16)
            acc_ref[pl.ds(at, KT), 0:HD] += lax.dot_general(ds, qs, nn, preferred_element_type=f32)
            acc_ref[pl.ds(at, KT), HD:2 * HD] += lax.dot_general(
                w, dos, nn, preferred_element_type=f32
            )
            dqt_ref[...] += lax.dot_general(kt_ref[t], ds, nn, preferred_element_type=f32)
            return carry

        lax.fori_loop(lo, hi, grads, 0)
        for h in range(GS):
            dq_ref[:, h * HD:(h + 1) * HD] = dqt_ref[:, h * BLK:(h + 1) * BLK].T.astype(bf16)

    block(own_ref, dq_own_ref, sc_ref[0])
    block(recv_ref, dq_recv_ref, sc_ref[1])
    part = length // 4
    for j in range(2):
        for z in range(4):
            at = pl.multiple_of(sc_ref[2 + j] * part + z * BLK, BLK)
            mine_ref[z, j] = acc_ref[pl.ds(at, BLK), :]
            at = pl.multiple_of(sc_ref[4 + j] * part + z * BLK, BLK)
            theirs_ref[z, j] = acc_ref[pl.ds(at, BLK), :].astype(bf16)


def attention(scalars, seg, own, recv, kv):
    length = kv.shape[0]
    rows = GS * BLK
    vmem = pl.BlockSpec(memory_space=pltpu.VMEM)
    return pl.pallas_call(
        attention_kernel,
        out_shape=(
            jax.ShapeDtypeStruct((BLK, rows), jnp.bfloat16),
            jax.ShapeDtypeStruct((BLK, rows), jnp.bfloat16),
            jax.ShapeDtypeStruct((4, 2, BLK, 2 * HD), jnp.float32),
            jax.ShapeDtypeStruct((4, 2, BLK, 2 * HD), jnp.bfloat16),
        ),
        in_specs=[pl.BlockSpec(memory_space=pltpu.SMEM), vmem, vmem, vmem, vmem],
        out_specs=(vmem, vmem, vmem, vmem),
        scratch_shapes=[
            pltpu.VMEM((length, rows), jnp.float32),
            pltpu.VMEM((length, rows), jnp.float32),
            pltpu.VMEM((length // KT, HD, KT), jnp.bfloat16),
            pltpu.VMEM((length, 2 * HD), jnp.float32),
            pltpu.VMEM((HD, rows), jnp.float32),
        ],
        compiler_params=pltpu.CompilerParams(vmem_limit_bytes=48 * 1024 * 1024),
        cost_estimate=pl.CostEstimate(
            flops=5_000_000_000, bytes_accessed=8_000_000, transcendentals=4_000_000
        ),
    )(scalars, seg, own, recv, kv)


def on_device(queries, key_states, value_states, out_grad, layer_input, segment_ids):
    f32 = jnp.float32
    bf16 = jnp.bfloat16
    y = lax.axis_index(YAX)
    z = lax.axis_index(Z)
    g = lax.axis_index(YH)
    half = GS * HD
    k, v = key_states[0], value_states[0]
    kv_groups = [
        jnp.concatenate([k[:, i * HD:(i + 1) * HD], v[:, i * HD:(i + 1) * HD]], axis=1)
        for i in range(GROUPS)
    ]
    to_send = jnp.concatenate(
        [jnp.broadcast_to(x[None], (8, BLK, 2 * HD)) for x in kv_groups], axis=0
    )
    kv = lax.all_to_all(to_send, CTX, 0, 0).reshape(16 * BLK, 2 * HD)

    def halves(at):
        return jnp.concatenate(
            [
                lax.dynamic_slice_in_dim(queries[0], at, half, 1),
                lax.dynamic_slice_in_dim(out_grad[0], at, half, 1),
            ],
            axis=0,
        )

    recv = lax.ppermute(halves((1 - g) * half), YAX, PARTNER)
    own = halves(g * half)

    features = layer_input.shape[2] // 8
    x_out = layer_input[0].reshape(BLK, 8, features).transpose(1, 0, 2)
    x_own = lax.all_to_all(x_out, FSDP, 0, 0)
    x_recv = lax.ppermute(x_own, YAX, PARTNER)

    middle = ((y == 1) | (y == 2)).astype(jnp.int32)
    scalars = jnp.stack(
        [
            (y * 4 + z) * BLK,
            ((3 - y) * 4 + z) * BLK,
            middle,
            3 - middle,
            1 - middle,
            2 + middle,
        ]
    ).astype(jnp.int32)
    dq_own, dq_recv, mine, theirs = attention(
        scalars, segment_ids.reshape(16, 128), own, recv, kv
    )
    dq_other = lax.ppermute(dq_recv, YAX, PARTNER)
    query_grad = jnp.where(
        g == 0,
        jnp.concatenate([dq_own, dq_other], axis=1),
        jnp.concatenate([dq_other, dq_own], axis=1),
    )

    from_neighbour = lax.ppermute(theirs, YAX, NEIGHBOUR)
    partial = (mine + from_neighbour.astype(f32)).astype(bf16)
    shares = lax.all_to_all(partial, Z, 0, 0)
    kv_grad = jnp.sum(shares.astype(f32), axis=0).astype(bf16)
    grad_own = lax.dynamic_index_in_dim(kv_grad, g, 0, keepdims=False)
    grad_partner = lax.dynamic_index_in_dim(kv_grad, 1 - g, 0, keepdims=False)
    grad_other = lax.ppermute(grad_partner, YAX, PARTNER)
    grads = [jnp.where(g == 0, grad_own, grad_other), jnp.where(g == 0, grad_other, grad_own)]
    key_grad = jnp.concatenate([x[:, :HD] for x in grads], axis=1)
    value_grad = jnp.concatenate([x[:, HD:] for x in grads], axis=1)

    both = jnp.stack([grad_own, grad_partner])
    gathered = lax.all_to_all(jnp.broadcast_to(both[None], (8,) + both.shape), FSDP, 0, 0)
    part = jnp.einsum("ftd,ftc->dc", x_own, gathered[:, 0], preferred_element_type=f32)
    part = part + jnp.einsum("ftd,ftc->dc", x_recv, gathered[:, 1], preferred_element_type=f32)
    pieces = part.astype(bf16).reshape(16, features // 16, 2 * HD)
    pieces = lax.all_to_all(pieces, (DP, YL, Z), 0, 0)
    tokens = BLK * 256
    piece = (jnp.sum(pieces.astype(f32), axis=0) * tokens ** (-0.5)).astype(bf16)
    whole = lax.all_to_all(jnp.broadcast_to(piece[None], (32,) + piece.shape), (DP, YH, YL, Z), 0, 0)
    whole = whole.reshape(2, 2, 8, features // 16, 2, HD).transpose(0, 2, 3, 4, 1, 5)
    weight_grad = whole.reshape(features, 4 * HD).astype(f32)
    return (query_grad[None], key_grad[None], value_grad[None], weight_grad)


def solution(mesh):
    devices = mesh.devices.reshape(2, 4, 2, 2, 2, 4)
    fine = Mesh(devices, (DP, FX, FC, YH, YL, Z))
    rows = (DP, FX, FC)
    in_specs = (
        P(rows, CTX, None),
        P(rows, CTX, None),
        P(rows, CTX, None),
        P(rows, CTX, None),
        P(rows, CTX, None),
        P(rows, None),
    )
    out_specs = (
        P(rows, CTX, None),
        P(rows, CTX, None),
        P(rows, CTX, None),
        P((FX, FC), None),
    )
    return jax.shard_map(
        on_device, mesh=fine, in_specs=in_specs, out_specs=out_specs, check_vma=False
    )
```

```python
import jax
import jax.numpy as jnp
from jax import lax
from jax.experimental import pallas as pl
from jax.experimental.pallas import tpu as pltpu
from jax.sharding import Mesh, PartitionSpec as P

HD = 128
GROUPS = 2
GS = 7
BLK = 128
KT = 256
LOG2E = 1.4426950408889634
SCALE = HD ** (-0.5)

DP, FX, FC, YH, YL, Z = "dp", "fx", "fc", "yh", "yl", "zh"
FSDP = (FX, FC)
YAX = (YH, YL)
CTX = (YH, YL, Z)
PARTNER = [(0, 3), (3, 0), (1, 2), (2, 1)]
NEIGHBOUR = [(0, 1), (1, 0), (2, 3), (3, 2)]
OPPOSITE = [(0, 2), (2, 0), (1, 3)]


def attention_kernel(
    sc_ref, seg_ref, own_ref, recv_ref, kv0_ref, kv1_ref, kv2_ref, kv3_ref, ahead_ref,
    dq_own_ref, dq_recv_ref, mine_ref, theirs_ref,
    s_ref, dp_ref, kt_ref, acc_ref, dqt_ref, kv_ref,
):
    del ahead_ref
    length = kv_ref.shape[0]
    for i, part_ref in enumerate((kv0_ref, kv1_ref, kv2_ref, kv3_ref)):
        for d in range(4):
            at = pl.multiple_of(sc_ref[6 + i] * (length // 4) + sc_ref[10 + d] * BLK, BLK)
            kv_ref[pl.ds(at, BLK), :] = part_ref[d]
    tiles = length // KT
    rows = GS * BLK
    nt = (((1,), (1,)), ((), ()))
    nn = (((1,), (0,)), ((), ()))
    f32 = jnp.float32
    bf16 = jnp.bfloat16
    seg = seg_ref[...]
    first = jnp.sum((seg < 1).astype(f32)).astype(jnp.int32)
    second = jnp.sum((seg < 2).astype(f32)).astype(jnp.int32)
    for t in range(tiles):
        kt_ref[t] = kv_ref[t * KT:(t + 1) * KT, 0:HD].T
    acc_ref[...] = jnp.zeros_like(acc_ref)

    def stack(ref, at):
        return jnp.concatenate(
            [ref[at * BLK:(at + 1) * BLK, h * HD:(h + 1) * HD] for h in range(GS)], axis=0
        )

    def block(src_ref, dq_ref, p0):
        qs = stack(src_ref, 0)
        dos = stack(src_ref, 1)
        qpos = p0 + lax.broadcasted_iota(jnp.int32, (1, BLK), 1)
        start = jnp.where(qpos >= second, second, jnp.where(qpos >= first, first, 0))
        low = jnp.where(p0 >= second, second, jnp.where(p0 >= first, first, 0))
        lo = low // KT
        hi = p0 // KT + 1

        def score(t, m):
            at = pl.multiple_of(t * KT, KT)
            k = kv_ref[pl.ds(at, KT), 0:HD]
            s = lax.dot_general(k, qs, nt, preferred_element_type=f32)
            kpos = at + lax.broadcasted_iota(jnp.int32, (KT, BLK), 0)
            seen = (kpos >= start) & (kpos <= qpos)
            s = jnp.concatenate(
                [jnp.where(seen, s[:, h * BLK:(h + 1) * BLK], -jnp.inf) for h in range(GS)], axis=1
            )
            s_ref[pl.ds(at, KT), :] = s
            return jnp.maximum(m, jnp.max(s, axis=0, keepdims=True))

        m = lax.fori_loop(lo, hi, score, jnp.full((1, rows), -jnp.inf, f32))

        def soft(t, carry):
            total, dot = carry
            at = pl.multiple_of(t * KT, KT)
            p = jnp.exp2((s_ref[pl.ds(at, KT), :] - m) * (SCALE * LOG2E))
            v = kv_ref[pl.ds(at, KT), HD:2 * HD]
            dp = lax.dot_general(v, dos, nt, preferred_element_type=f32)
            s_ref[pl.ds(at, KT), :] = p
            dp_ref[pl.ds(at, KT), :] = dp
            total = total + jnp.sum(p, axis=0, keepdims=True)
            dot = dot + jnp.sum(p * dp, axis=0, keepdims=True)
            return total, dot

        zero = jnp.zeros((1, rows), f32)
        total, dot = lax.fori_loop(lo, hi, soft, (zero, zero))
        inv = 1.0 / total
        delta = dot * inv
        inv_scaled = inv * SCALE
        dqt_ref[...] = jnp.zeros_like(dqt_ref)

        def grads(t, carry):
            at = pl.multiple_of(t * KT, KT)
            p = s_ref[pl.ds(at, KT), :]
            w = (p * inv).astype(bf16)
            ds = (p * (dp_ref[pl.ds(at, KT), :] - delta) * inv_scaled).astype(bf16)
            acc_ref[pl.ds(at, KT), 0:HD] += lax.dot_general(ds, qs, nn, preferred_element_type=f32)
            acc_ref[pl.ds(at, KT), HD:2 * HD] += lax.dot_general(
                w, dos, nn, preferred_element_type=f32
            )
            dqt_ref[...] += lax.dot_general(kt_ref[t], ds, nn, preferred_element_type=f32)
            return carry

        lax.fori_loop(lo, hi, grads, 0)
        for h in range(GS):
            dq_ref[:, h * HD:(h + 1) * HD] = dqt_ref[:, h * BLK:(h + 1) * BLK].T.astype(bf16)

    block(own_ref, dq_own_ref, sc_ref[0])
    block(recv_ref, dq_recv_ref, sc_ref[1])
    part = length // 4
    for j in range(2):
        for z in range(4):
            at = pl.multiple_of(sc_ref[2 + j] * part + z * BLK, BLK)
            mine_ref[z, j] = acc_ref[pl.ds(at, BLK), :]
            at = pl.multiple_of(sc_ref[4 + j] * part + z * BLK, BLK)
            theirs_ref[z, j] = acc_ref[pl.ds(at, BLK), :].astype(bf16)


def split_kernel(sc_ref, a_ref, b_ref, c_ref, d_ref, own_ref, other_ref):
    def write(first, second):
        for i, ref in enumerate((a_ref, b_ref, c_ref, d_ref)):
            for out, g in ((first, 0), (second, 1)):
                out[i, :, 0:HD] = ref[:, g * HD:(g + 1) * HD]
                out[i, :, HD:2 * HD] = ref[:, (2 + g) * HD:(3 + g) * HD]

    @pl.when(sc_ref[0] == 0)
    def _():
        write(own_ref, other_ref)

    @pl.when(sc_ref[0] != 0)
    def _():
        write(other_ref, own_ref)


def split_groups(group, blocks):
    vmem = pl.BlockSpec(memory_space=pltpu.VMEM)
    shape = jax.ShapeDtypeStruct((4, BLK, 2 * HD), jnp.bfloat16)
    return pl.pallas_call(
        split_kernel,
        out_shape=(shape, shape),
        in_specs=[pl.BlockSpec(memory_space=pltpu.SMEM)] + [vmem] * 4,
        out_specs=(vmem, vmem),
    )(group, *blocks)


def attention(scalars, seg, own, recv, kvs, ahead):
    length = 4 * kvs[0].shape[0] * kvs[0].shape[1]
    rows = GS * BLK
    vmem = pl.BlockSpec(memory_space=pltpu.VMEM)
    return pl.pallas_call(
        attention_kernel,
        out_shape=(
            jax.ShapeDtypeStruct((BLK, rows), jnp.bfloat16),
            jax.ShapeDtypeStruct((BLK, rows), jnp.bfloat16),
            jax.ShapeDtypeStruct((4, 2, BLK, 2 * HD), jnp.float32),
            jax.ShapeDtypeStruct((4, 2, BLK, 2 * HD), jnp.bfloat16),
        ),
        in_specs=[pl.BlockSpec(memory_space=pltpu.SMEM)] + [vmem] * 7 + [pl.BlockSpec(memory_space=pl.ANY)],
        out_specs=(vmem, vmem, vmem, vmem),
        scratch_shapes=[
            pltpu.VMEM((length, rows), jnp.float32),
            pltpu.VMEM((length, rows), jnp.float32),
            pltpu.VMEM((length // KT, HD, KT), jnp.bfloat16),
            pltpu.VMEM((length, 2 * HD), jnp.float32),
            pltpu.VMEM((HD, rows), jnp.float32),
            pltpu.VMEM((length, 2 * HD), jnp.bfloat16),
        ],
        compiler_params=pltpu.CompilerParams(vmem_limit_bytes=48 * 1024 * 1024),
        cost_estimate=pl.CostEstimate(
            flops=5_000_000_000, bytes_accessed=8_000_000, transcendentals=4_000_000
        ),
    )(scalars, seg, own, recv, *kvs, ahead)


def on_device(queries, key_states, value_states, out_grad, layer_input, segment_ids):
    f32 = jnp.float32
    bf16 = jnp.bfloat16
    y = lax.axis_index(YAX)
    z = lax.axis_index(Z)
    g = lax.axis_index(YH)
    half = GS * HD
    raw = jnp.concatenate([key_states[0], value_states[0]], axis=1)
    around = [raw] + [lax.ppermute(raw, Z, [(i, (i + d) % 4) for i in range(4)]) for d in (1, 2, 3)]
    kv_own, kv_other = split_groups(g.astype(jnp.int32)[None], around)
    kvs = (
        kv_own,
        lax.ppermute(kv_other, YAX, OPPOSITE),
        lax.ppermute(kv_other, YAX, PARTNER),
        lax.ppermute(kv_own, YAX, [(0, 1), (1, 0), (2, 3)]),
    )

    def halves(at):
        return jnp.concatenate(
            [
                lax.dynamic_slice_in_dim(queries[0], at, half, 1),
                lax.dynamic_slice_in_dim(out_grad[0], at, half, 1),
            ],
            axis=0,
        )

    recv = lax.ppermute(halves((1 - g) * half), YAX, PARTNER)
    own = halves(g * half)

    features = layer_input.shape[2] // 8
    x_out = layer_input[0].reshape(BLK, 8, features).transpose(1, 0, 2)
    x_own = lax.all_to_all(x_out, FSDP, 0, 0)
    x_recv = lax.ppermute(x_own, YAX, PARTNER)
    fx = lax.axis_index(FX)
    fc = lax.axis_index(FC)

    def arranged(core):
        rows = [
            lax.dynamic_index_in_dim(x, ((fx - d) % 4) * 2 + core, 0, keepdims=False)
            for d in range(4)
            for x in (x_own, x_recv)
        ]
        return jnp.stack(rows)

    x_near = arranged(fc)
    x_far = arranged(1 - fc)

    middle = ((y == 1) | (y == 2)).astype(jnp.int32)
    scalars = jnp.stack(
        [
            (y * 4 + z) * BLK,
            ((3 - y) * 4 + z) * BLK,
            middle,
            3 - middle,
            1 - middle,
            2 + middle,
            y,
            (y + 2) % 4,
            3 - y,
            y + 1 - 2 * (y % 2),
            z,
            (z + 3) % 4,
            (z + 2) % 4,
            (z + 1) % 4,
        ]
    ).astype(jnp.int32)
    dq_own, dq_recv, mine, theirs = attention(
        scalars, segment_ids.reshape(16, 128), own, recv, kvs, x_own
    )
    dq_other = lax.ppermute(dq_recv, YAX, PARTNER)
    query_grad = jnp.where(
        g == 0,
        jnp.concatenate([dq_own, dq_other], axis=1),
        jnp.concatenate([dq_other, dq_own], axis=1),
    )

    from_neighbour = lax.ppermute(theirs, YAX, NEIGHBOUR)
    partial = (mine + from_neighbour.astype(f32)).astype(bf16)
    total = lax.dynamic_index_in_dim(partial, z, 0, keepdims=False).astype(f32)
    for d in (1, 2, 3):
        piece = lax.dynamic_index_in_dim(partial, (z + d) % 4, 0, keepdims=False)
        piece = lax.ppermute(piece, Z, [(i, (i + d) % 4) for i in range(4)])
        total = total + piece.astype(f32)
    kv_grad = total.astype(bf16)
    grad_own = lax.dynamic_index_in_dim(kv_grad, g, 0, keepdims=False)
    grad_partner = lax.dynamic_index_in_dim(kv_grad, 1 - g, 0, keepdims=False)
    grad_other = lax.ppermute(grad_partner, YAX, PARTNER)
    grads = [jnp.where(g == 0, grad_own, grad_other), jnp.where(g == 0, grad_other, grad_own)]
    key_grad = jnp.concatenate([x[:, :HD] for x in grads], axis=1)
    value_grad = jnp.concatenate([x[:, HD:] for x in grads], axis=1)

    both = jnp.stack([grad_own, grad_partner])
    near = jnp.concatenate(
        [both] + [lax.ppermute(both, FX, [(i, (i + d) % 4) for i in range(4)]) for d in (1, 2, 3)]
    )
    far = lax.ppermute(near, FC, [(0, 1), (1, 0)])
    part = jnp.einsum("etd,etc->dc", x_near, near, preferred_element_type=f32)
    part = part + jnp.einsum("etd,etc->dc", x_far, far, preferred_element_type=f32)
    pieces = part.astype(bf16).reshape(16, features // 16, 2 * HD)
    pieces = lax.all_to_all(pieces, (DP, YL, Z), 0, 0)
    tokens = BLK * 256
    piece = (jnp.sum(pieces.astype(f32), axis=0) * tokens ** (-0.5)).astype(bf16)
    whole = lax.all_to_all(jnp.broadcast_to(piece[None], (32,) + piece.shape), (DP, YH, YL, Z), 0, 0)
    whole = whole.reshape(2, 2, 8, features // 16, 2, HD).transpose(0, 2, 3, 4, 1, 5)
    weight_grad = whole.reshape(features, 4 * HD).astype(f32)
    return (query_grad[None], key_grad[None], value_grad[None], weight_grad)


def solution(mesh):
    devices = mesh.devices.reshape(2, 4, 2, 2, 2, 4)
    fine = Mesh(devices, (DP, FX, FC, YH, YL, Z))
    rows = (DP, FX, FC)
    in_specs = (
        P(rows, CTX, None),
        P(rows, CTX, None),
        P(rows, CTX, None),
        P(rows, CTX, None),
        P(rows, CTX, None),
        P(rows, None),
    )
    out_specs = (
        P(rows, CTX, None),
        P(rows, CTX, None),
        P(rows, CTX, None),
        P((FX, FC), None),
    )
    return jax.shard_map(
        on_device, mesh=fine, in_specs=in_specs, out_specs=out_specs, check_vma=False
    )
```
